256 devices in a mesh: row: 8 (over x, core), col: 16 (over z_lo, y), depth: 2 (over z_hi).
Axes of the slice: x: 4, y: 4, z: 8 (z_hi: 2, z_lo: 4; z = z_hi * 4 + z_lo), core: 2. Of those that a mesh axis runs over, the one named last changes fastest.
Arguments:
- activations: bfloat16 [2, 1024, 8192], P('depth', 'col', 'row'), may hold values from -6 to 6
- weight_tiles: bfloat16 [8, 16, 56, 128, 128], P('row', 'col'), may hold values from -0.09375 to 0.09375
- tile_rows: int32 [8, 16, 56], P('row', 'col'), may hold values from 0 to 7, as said below
- tile_cols: int32 [8, 16, 56], P('row', 'col'), may hold values from 0 to 13, as said below
- grad_out: bfloat16 [2, 1024, 28672], P('depth', 'row', 'col'), may hold values from -6 to 6
Outputs:
- output: bfloat16 [2, 1024, 28672], P('depth', 'row', 'col')
- grad_input: bfloat16 [2, 1024, 8192], P('depth', 'col', 'row')
- grad_tiles: float32 [8, 16, 56, 128, 128], P('row', 'col')
The draws below stay inside these ranges and needn't reach their ends.
Inputs may be any that keep to these rules, and one draw needn't show every extreme that they name: For each block (i, j), the pairs (tile_rows[i, j, k], tile_cols[i, j, k]) over k are 56 distinct tiles of the block's 8 x 14 grid, in increasing order of tile_rows * 14 + tile_cols. `tile_cols`: drawn together with tile_rows, as stated there.
All inputs are finite; a program needn't handle non-finite values.
Results may differ from the reference program's by a relative error of at most 0.001.
Values may be sent and summed in bfloat16 or wider, within the bound.
A program may use at most 128 MiB of HBM per device.

```python
import math
import jax
import jax.numpy as jnp
from jax import lax

D = 8192
FF = 28672
TILE_SIZE = 128
TOK_GROUP = 1024
TILE_ROWS = 8
TILE_COLS = 14
KEPT_TILES = 56
N_ROW = 8
N_COL = 16
N_DEPTH = 2


def kept_lists(key):
    block_tiles = TILE_ROWS * TILE_COLS
    subkeys = jax.random.split(jax.random.fold_in(key, 11), N_ROW * N_COL)

    def pick_tiles(subkey):
        return jax.random.permutation(subkey, block_tiles)[:KEPT_TILES]
    chosen = jnp.sort(jax.vmap(pick_tiles)(subkeys), axis=1)
    return chosen.reshape(N_ROW, N_COL, KEPT_TILES).astype(jnp.int32)


def draw_tile_rows(key, part):
    return kept_lists(key) // TILE_COLS


def draw_tile_cols(key, part):
    return kept_lists(key) % TILE_COLS


def level_of(key, extent, pieces, smallest, top_value):
    def one(dim, parts):
        draws = jax.random.uniform(jax.random.fold_in(jax.random.fold_in(key, 6), dim), (parts,), jnp.float32, smallest / len(pieces), top_value / len(pieces))
        return jnp.repeat(jnp.exp(draws), extent[dim] // parts).reshape((-1,) + (1,) * (len(extent) - dim - 1))

    gain = one(*pieces[0])
    for cut in pieces[1:]:
        gain = gain * one(*cut)
    return gain


def normal_values(own_key, dims, width, limit, cuts=(), kind=jnp.bfloat16):
    level = level_of(own_key, dims, cuts, -0.22, 0.18) if cuts else 1.0
    drawn = jax.random.normal(own_key, dims, jnp.float32) * width * level
    return jnp.minimum(jnp.maximum(drawn, -limit), limit).astype(kind)


def setup_inputs(seed: int = 0) -> dict:
    streams_of = jax.random.split(jax.random.key(seed), 6)
    activations = normal_values(streams_of[0], (N_DEPTH, TOK_GROUP, D), 1.0, 6.0, ((0, 2), (1, 16), (2, 8)))
    weight_tiles = normal_values(streams_of[1], (N_ROW, N_COL, KEPT_TILES, TILE_SIZE, TILE_SIZE), (D // 2) ** -0.5, 0.09375, ((0, 8), (1, 16)))
    tile_rows = draw_tile_rows(jax.random.fold_in(streams_of[5], 71), 0)
    tile_cols = draw_tile_cols(jax.random.fold_in(streams_of[5], 71), 0)
    grad_out = normal_values(streams_of[4], (N_DEPTH, TOK_GROUP, FF), 1.0, 6.0, ((0, 2), (1, 8), (2, 16)))
    return {"activations": activations, "weight_tiles": weight_tiles, "tile_rows": tile_rows, "tile_cols": tile_cols, "grad_out": grad_out}


def reference(activations, weight_tiles, tile_rows, tile_cols, grad_out):
    groups = activations.shape[0]
    group_tokens = activations.shape[1]
    all_tokens = groups * group_tokens
    flat_input = activations.reshape(all_tokens, D)
    flat_grad = grad_out.reshape(all_tokens, FF)
    block_rows = D // N_ROW
    block_cols = FF // N_COL
    grad_scale = math.sqrt(all_tokens)

    def column_step(input_grad, column_index):
        grad_block = lax.dynamic_slice_in_dim(flat_grad, column_index * block_cols, block_cols, 1)
        grad_block = grad_block.astype(jnp.float32).reshape(all_tokens, TILE_COLS, TILE_SIZE)

        def row_step(carry, row_index):
            out_total, input_total = carry
            kept_weights = weight_tiles[row_index, column_index].astype(jnp.float32)
            rows_here = tile_rows[row_index, column_index]
            cols_here = tile_cols[row_index, column_index]
            input_block = lax.dynamic_slice_in_dim(flat_input, row_index * block_rows, block_rows, 1)
            input_block = input_block.astype(jnp.float32).reshape(all_tokens, TILE_ROWS, TILE_SIZE)
            input_kept = jnp.take(input_block, rows_here, axis=1)
            grad_kept = jnp.take(grad_block, cols_here, axis=1)
            forward = jnp.einsum('tkb,kbj->ktj', input_kept, kept_weights)
            forward = jax.ops.segment_sum(forward, cols_here, num_segments=TILE_COLS)
            out_total = out_total + forward.transpose(1, 0, 2).reshape(all_tokens, block_cols)
            backward = jnp.einsum('tkj,kbj->ktb', grad_kept, kept_weights)
            backward = jax.ops.segment_sum(backward, rows_here, num_segments=TILE_ROWS)
            backward = backward.transpose(1, 0, 2).reshape(all_tokens, block_rows)
            before = lax.dynamic_slice_in_dim(input_total, row_index * block_rows, block_rows, 1)
            input_total = lax.dynamic_update_slice_in_dim(input_total, before + backward, row_index * block_rows, 1)
            tile_grad = jnp.einsum('tkb,tkj->kbj', input_kept, grad_kept) / grad_scale
            return ((out_total, input_total), tile_grad)
        start_carry = (jnp.zeros((all_tokens, block_cols), jnp.float32), input_grad)
        (out_total, input_grad), tile_grads = lax.scan(row_step, start_carry, jnp.arange(N_ROW, dtype=jnp.int32))
        return (input_grad, (out_total.astype(jnp.bfloat16), tile_grads))
    input_grad, (column_outs, column_grads) = lax.scan(column_step, jnp.zeros((all_tokens, D), jnp.float32), jnp.arange(N_COL, dtype=jnp.int32))
    output = column_outs.transpose(1, 0, 2).reshape(groups, group_tokens, FF)
    grad_input = input_grad.astype(jnp.bfloat16).reshape(groups, group_tokens, D)
    grad_tiles = column_grads.transpose(1, 0, 2, 3, 4)
    return (output, grad_input, grad_tiles)
```

```python
import functools
import math

import jax
import jax.numpy as jnp
from jax import lax
from jax.experimental import pallas as pl
from jax.experimental.pallas import tpu as pltpu
from jax.sharding import PartitionSpec as P

MESH = pl.DeviceIdType.MESH
T = 128
F32 = jnp.float32
NSEM = 128


def kernel(
    act, wt, rows, cols, gout,
    y_out, dx_out, dw_out,
    xall, gall, xst, gst, tiles, wd, dwd, dwt,
    dpart, dra, drb, drc, drd, dsum, dmine, zrecv,
    ypart, pair, ya, yb, yc, yd,
    ss, rs, ls, zss, zrs,
):
    r, c, d = lax.axis_index("row"), lax.axis_index("col"), lax.axis_index("depth")
    x, k, y, zl = r // 2, r % 2, c % 4, c // 4
    z = d * 4 + zl
    od = 1 - d

    def dev(dx=0, dk=0, dy=0, dz=0):
        zz = (z + dz + 8) % 8
        return {
            "row": ((x + dx + 4) % 4) * 2 + (k + dk) % 2,
            "col": (zz % 4) * 4 + (y + dy + 4) % 4,
            "depth": zz // 4,
        }

    def xs(zz, yy, lo=0, n=64):
        return xall.at[pl.ds(pl.multiple_of((zz * 4 + yy) * 64 + lo, 32), n)]

    def gs(dd, xx, kk, lo=0, n=128):
        return gall.at[pl.ds(pl.multiple_of(dd * 1024 + (xx * 2 + kk) * 128 + lo, 64), n)]

    zm = [(z + j + 8) % 8 for j in range(-4, 5)]
    zat = lambda j: zm[j + 4]
    yat = lambda j: (y + j + 4) % 4
    xat = lambda j: (x + j + 4) % 4

    ids = {}
    sent = {}

    def sem(name):
        if name not in ids:
            ids[name] = len(ids)
        return ids[name]

    def desc(name, src, dst, device):
        i = sem(name)
        return pltpu.make_async_remote_copy(
            src, dst, ss.at[i], rs.at[i], device_id=device, device_id_type=MESH
        )

    def send(name, make):
        desc(name, *make()).start()
        sent.setdefault(name, make)

    def recv(name, ref):
        desc(name, ref, ref, dev(dk=1)).wait_recv()

    local = [
        pltpu.make_async_copy(act.at[0], xs(z, y), ls.at[0]),
        pltpu.make_async_copy(gout.at[0], gs(d, x, k), ls.at[1]),
        pltpu.make_async_copy(wt.at[0, 0], tiles.at[pl.ds(0, 56)], ls.at[2]),
    ]
    for cp in local:
        cp.start()

    barrier = pltpu.get_barrier_semaphore()
    peers = [dev(dx=1), dev(dx=-1), dev(dk=1), dev(dy=1), dev(dy=-1)]
    peers += [dev(dz=j) for j in range(1, 8)]
    for peer in peers:
        pl.semaphore_signal(barrier, inc=1, device_id=peer, device_id_type=MESH)
    pl.semaphore_wait(barrier, len(peers))

    def z_send(h):
        if h < 3:
            up, down = zat(-h), zat(h)
            send(f"zu{h}", lambda: (act.at[0] if h == 0 else xs(up, y), xs(up, y), dev(dz=1)))
            send(f"zd{h}", lambda: (act.at[0] if h == 0 else xs(down, y), xs(down, y), dev(dz=-1)))
        else:
            send("zu3", lambda: (xs(zat(-3), y, 0, 32), xs(zat(-3), y, 0, 32), dev(dz=1)))
            send("zd3", lambda: (xs(zat(3), y, 32, 32), xs(zat(3), y, 32, 32), dev(dz=-1)))

    def z_recv(h):
        if h < 4:
            recv(f"zu{h - 1}", xs(zat(-h), y))
            recv(f"zd{h - 1}", xs(zat(h), y))
        else:
            recv("zu3", xs(zat(4), y, 0, 32))
            recv("zd3", xs(zat(4), y, 32, 32))

    def y_send(j, src=None):
        zz = zat(j)
        send(f"yu{j}", lambda: (xs(zz, y) if src is None else src, xs(zz, y), dev(dy=1)))
        send(f"yd{j}", lambda: (xs(zz, y) if src is None else src, xs(zz, y), dev(dy=-1)))

    def y_forward(j):
        zz = zat(j)
        recv(f"yu{j}", xs(zz, yat(-1)))
        send(f"yU{j}", lambda: (xs(zz, yat(-1), 0, 32), xs(zz, yat(-1), 0, 32), dev(dy=1)))
        recv(f"yd{j}", xs(zz, yat(1)))
        send(f"yD{j}", lambda: (xs(zz, yat(1), 32, 32), xs(zz, yat(1), 32, 32), dev(dy=-1)))

    def y_last(j):
        zz = zat(j)
        recv(f"yU{j}", xs(zz, yat(2), 0, 32))
        recv(f"yD{j}", xs(zz, yat(2), 32, 32))

    def both(h, own, do):
        if own:
            do(h)
            do(-h)

    def g_send(tag, dd, src):
        send(f"gk0{tag}", lambda: (src, gs(dd, x, k), dev(dk=1)))
        send(f"gu{tag}", lambda: (src, gs(dd, x, k), dev(dx=1)))
        send(f"gd{tag}", lambda: (src, gs(dd, x, k), dev(dx=-1)))

    def g_forward(tag, dd):
        left, right = xat(-1), xat(1)
        recv(f"gu{tag}", gs(dd, left, k))
        send(f"gU{tag}", lambda: (gs(dd, left, k, 0, 64), gs(dd, left, k, 0, 64), dev(dx=1)))
        send(f"gk1{tag}", lambda: (gs(dd, left, k), gs(dd, left, k), dev(dk=1)))
        recv(f"gd{tag}", gs(dd, right, k))
        send(f"gD{tag}", lambda: (gs(dd, right, k, 64, 64), gs(dd, right, k, 64, 64), dev(dx=-1)))
        send(f"gk3{tag}", lambda: (gs(dd, right, k), gs(dd, right, k), dev(dk=1)))

    def g_last(tag, dd):
        far = xat(2)
        recv(f"gU{tag}", gs(dd, far, k, 0, 64))
        recv(f"gD{tag}", gs(dd, far, k, 64, 64))
        send(f"gk2{tag}", lambda: (gs(dd, far, k), gs(dd, far, k), dev(dk=1)))

    def g_core(tag, dd, j):
        xx = {0: x, 1: xat(-1), 2: xat(2), 3: xat(1)}[j]
        recv(f"gk{j}{tag}", gs(dd, xx, 1 - k))

    def g_stage(j):
        base = pl.multiple_of(d * 1024 + xat(j) * 256, 256)
        return pltpu.make_async_copy(gall.at[pl.ds(base, 256)], gst[j % 4], ls.at[8 + j % 4])

    def dx_compute(j):
        g_stage(j).start()
        g_stage(j).wait()

        @pl.loop(0, 4)
        def _(n):
            cut = pl.ds(pl.multiple_of(n * 256, 256), 256)
            dpart[j % 4][:, cut] = lax.dot_general(
                gst[j % 4][...], wd[cut, :],
                (((1,), (1,)), ((), ())), preferred_element_type=F32,
            )

    def dblock(q, j, half):
        return dpart[q % 4].at[pl.ds(pl.multiple_of(yat(j) * 64, 64), 64), pl.ds(half * 512, 512)]

    def dx_send(j):
        p = xat(j)
        send(f"da{j}", lambda: (dblock(j, 2, 0), dra[j % 4], dev(dy=1)))
        send(f"db{j}", lambda: (dblock(j, 2, 1), drb[j % 4], dev(dy=-1)))
        send(f"dc1{j}", lambda: (dblock(j, 1, 1), drc[j % 4][1], dev(dy=1)))
        send(f"dd0{j}", lambda: (dblock(j, -1, 0), drd[j % 4][0], dev(dy=-1)))

    def dx_middle(j):
        p = xat(j)
        recv(f"da{j}", dra[j % 4])
        dra[j % 4][...] += dblock(j, 1, 0)[...]
        send(f"dc0{j}", lambda: (dra[j % 4], drc[j % 4][0], dev(dy=1)))
        recv(f"db{j}", drb[j % 4])
        drb[j % 4][...] += dblock(j, -1, 1)[...]
        send(f"dd1{j}", lambda: (drb[j % 4], drd[j % 4][1], dev(dy=-1)))

    def dx_last(j):
        p = xat(j)
        for half in (1, 0):
            recv(f"dc{half}{j}", drc[j % 4][half])
            recv(f"dd{1 - half}{j}", drd[j % 4][1 - half])
        for half in range(2):
            dsum[j % 4][:, half * 512:half * 512 + 512] = (
                dblock(j, 0, half)[...] + drc[j % 4][half][...] + drd[j % 4][half][...]
            )

        @pl.when(p == zl)
        def _():
            dmine[...] = dsum[j % 4][...]

        @pl.when(p != zl)
        def _():
            slot = (zl - p + 4) % 4 - 1
            pltpu.make_async_remote_copy(
                dsum[j % 4], zrecv.at[slot], zss.at[slot], zrs.at[slot],
                device_id={"row": r, "col": p * 4 + y, "depth": d}, device_id_type=MESH,
            ).start()

    def x_stage(j):
        base = pl.multiple_of(d * 1024 + xat(j) * 256, 256)
        return pltpu.make_async_copy(xall.at[pl.ds(base, 256)], xst[j % 4], ls.at[4 + j % 4])

    def y_compute(j):
        x_stage(j).wait()

        @pl.loop(0, 7)
        def _(n):
            cut = pl.ds(pl.multiple_of(n * 256, 256), 256)
            ypart[j % 4][:, cut] = jnp.dot(
                xst[j % 4][...], wd[:, cut], preferred_element_type=F32
            )

        send(f"p{j}", lambda: (ypart[j % 4].at[pl.ds(pl.multiple_of((1 - k) * 128, 128), 128)], pair[j % 4], dev(dk=1)))

    def yblock(j, half):
        return pair[j % 4].at[:, pl.ds(half * 896, 896)]

    def y_pair(j):
        recv(f"p{j}", pair[j % 4])
        pair[j % 4][...] += ypart[j % 4][pl.ds(pl.multiple_of(k * 128, 128), 128), :]

    local[2].wait()
    tiles[56] = jnp.zeros((T, T), jnp.bfloat16)

    g_send("o", d, gout.at[0])
    z_send(0)
    y_send(0, act.at[0])

    def fill(i, at):
        for j in range(14):
            cell = i * 14 + j
            here = jnp.minimum(at, 55)
            hit = jnp.logical_and(at < 56, rows[0, 0, here] * 14 + cols[0, 0, here] == cell)
            wd[pl.ds(pl.multiple_of(i * T, T), T), j * T:j * T + T] = tiles[jnp.where(hit, at, 56)]
            at = at + hit.astype(jnp.int32)
        return at

    lax.fori_loop(0, 8, fill, jnp.int32(0))

    z_recv(1)
    z_send(1)
    both(1, True, y_send)
    y_forward(0)
    local[1].wait()
    g_core("o", d, 0)
    dx_compute(0)
    z_recv(2)
    z_send(2)
    both(2, True, y_send)
    dx_send(0)
    both(1, True, y_forward)
    z_recv(3)
    z_send(3)
    both(3, True, y_send)
    send("gz0", lambda: (gout.at[0, pl.ds(0, 64)], gs(d, x, k, 0, 64), dev(dz=4)))
    send("gz1", lambda: (gout.at[0, pl.ds(64, 64)], gs(d, x, k, 64, 64), dev(dz=4)))
    both(2, True, y_forward)
    g_forward("o", d)
    both(3, True, y_forward)
    g_core("o", d, 1)
    dx_compute(-1)
    dx_send(-1)
    g_core("o", d, 3)
    dx_compute(1)
    dx_send(1)
    dx_middle(0)
    local[0].wait()
    y_last(0)
    for h in (1, 2, 3):
        both(h, True, y_last)
    for j in (2, 1, -1, 0):
        x_stage(j).start()
    y_compute(2)
    y_compute(1)
    y_pair(2)
    send("oa", lambda: (yblock(2, 0), ya, dev(dx=1)))
    send("ob", lambda: (yblock(2, 1), yb, dev(dx=-1)))
    y_compute(-1)
    y_pair(1)
    send("oc1", lambda: (yblock(1, 1), yc[1], dev(dx=1)))
    y_pair(-1)
    send("od0", lambda: (yblock(-1, 0), yd[0], dev(dx=-1)))
    g_last("o", d)
    g_core("o", d, 2)
    dx_compute(2)
    dx_send(2)
    z_recv(4)
    for h in (1, 2, 3):
        both(h, False, y_send)
    y_send(4)
    y_compute(0)
    recv("gz0", gs(od, x, k, 0, 64))
    recv("gz1", gs(od, x, k, 64, 64))
    g_send("t", od, gs(od, x, k))
    dx_middle(-1)
    dx_middle(1)
    recv("oa", ya)
    ya[...] += yblock(1, 0)[...]
    send("oc0", lambda: (ya, yc[0], dev(dx=1)))
    recv("ob", yb)
    yb[...] += yblock(-1, 1)[...]
    send("od1", lambda: (yb, yd[1], dev(dx=-1)))

    def dw_compute(dd, first):
        base = pl.multiple_of(dd * 1024, 1024)

        @pl.loop(0, 7)
        def _(n):
            cut = pl.ds(pl.multiple_of(n * 256, 256), 256)
            got = lax.dot_general(
                xall[pl.ds(base, 1024), :], gall[pl.ds(base, 1024), cut],
                (((0,), (0,)), ((), ())), preferred_element_type=F32,
            )
            for i in range(8):
                for j in range(2):
                    part = got[i * T:i * T + T, j * T:j * T + T]
                    at = i * 14 + n * 2 + j
                    dwd[at] = part if first else dwd[at] + part

    dx_last(0)
    dw_compute(d, True)
    dx_middle(2)
    dx_last(-1)
    dx_last(1)
    for h in (1, 2, 3):
        both(h, False, y_forward)
    y_forward(4)
    g_forward("t", od)
    dx_last(2)
    y_pair(0)
    g_last("t", od)
    for h in (1, 2, 3):
        both(h, False, y_last)
    y_last(4)
    for j in range(4):
        g_core("t", od, j)
    dw_compute(od, False)

    scale = 1.0 / math.sqrt(2048.0)

    @pl.loop(0, 8)
    def _(n):
        for i in range(7):
            t = n * 7 + i
            dwt[t] = dwd[rows[0, 0, t] * 14 + cols[0, 0, t]] * scale

    out = pltpu.make_async_copy(dwt, dw_out.at[0, 0], ls.at[3])
    out.start()
    for half in range(2):
        recv(f"oc{1 - half}", yc[1 - half])
        recv(f"od{half}", yd[half])
    for half in range(2):
        y_out[0, :, half * 896:half * 896 + 896] = (
            yblock(0, half)[...] + yc[half][...] + yd[half][...]
        ).astype(jnp.bfloat16)
    for slot in range(3):
        pltpu.make_async_remote_copy(
            zrecv.at[slot], zrecv.at[slot], zss.at[slot], zrs.at[slot],
            device_id=dev(dk=1), device_id_type=MESH,
        ).wait()
    dx_out[0] = (dmine[...] + zrecv[0] + zrecv[1] + zrecv[2]).astype(jnp.bfloat16)
    out.wait()
    for name, make in sent.items():
        desc(name, *make()).wait_send()


def shards(act, wt, rows, cols, gout):
    hbm = pl.BlockSpec(memory_space=pl.ANY)
    smem = pl.BlockSpec(memory_space=pltpu.SMEM)
    vmem = pl.BlockSpec(memory_space=pltpu.VMEM)
    bf16 = jnp.bfloat16
    dma = pltpu.SemaphoreType.DMA
    return tuple(
        pl.pallas_call(
            kernel,
            out_shape=[
                jax.ShapeDtypeStruct((1, 128, 1792), bf16),
                jax.ShapeDtypeStruct((1, 64, 1024), bf16),
                jax.ShapeDtypeStruct((1, 1, 56, T, T), F32),
            ],
            in_specs=[hbm, hbm, smem, smem, hbm],
            out_specs=[vmem, vmem, hbm],
            scratch_shapes=[
                pltpu.VMEM((2048, 1024), bf16),
                pltpu.VMEM((2048, 1792), bf16),
                [pltpu.VMEM((256, 1024), bf16)] * 4,
                [pltpu.VMEM((256, 1792), bf16)] * 4,
                pltpu.VMEM((57, T, T), bf16),
                pltpu.VMEM((1024, 1792), bf16),
                pltpu.VMEM((112, T, T), F32),
                pltpu.VMEM((56, T, T), F32),
                [pltpu.VMEM((256, 1024), F32)] * 4,
                [pltpu.VMEM((64, 512), F32)] * 4,
                [pltpu.VMEM((64, 512), F32)] * 4,
                [[pltpu.VMEM((64, 512), F32)] * 2] * 4,
                [[pltpu.VMEM((64, 512), F32)] * 2] * 4,
                [pltpu.VMEM((64, 1024), F32)] * 4,
                pltpu.VMEM((64, 1024), F32),
                pltpu.VMEM((3, 64, 1024), F32),
                [pltpu.VMEM((256, 1792), F32)] * 4,
                [pltpu.VMEM((128, 1792), F32)] * 4,
                pltpu.VMEM((128, 896), F32),
                pltpu.VMEM((128, 896), F32),
                [pltpu.VMEM((128, 896), F32)] * 2,
                [pltpu.VMEM((128, 896), F32)] * 2,
                dma((NSEM,)), dma((NSEM,)), dma((12,)), dma((3,)), dma((3,)),
            ],
            compiler_params=pltpu.CompilerParams(
                collective_id=0, has_side_effects=True, vmem_limit_bytes=62 * 2**20
            ),
        )(act, wt, rows, cols, gout)
    )


def solution(mesh):
    placed = (
        P("depth", "col", "row"),
        P("row", "col", None, None, None),
        P("row", "col", None),
        P("row", "col", None),
        P("depth", "row", "col"),
    )
    return jax.shard_map(
        shards,
        mesh=mesh,
        in_specs=placed,
        out_specs=(
            P("depth", "row", "col"),
            P("depth", "col", "row"),
            P("row", "col", None, None, None),
        ),
        check_vma=False,
    )
```

```python
import functools
import math

import jax
import jax.numpy as jnp
from jax import lax
from jax.experimental import pallas as pl
from jax.experimental.pallas import tpu as pltpu
from jax.sharding import PartitionSpec as P

MESH = pl.DeviceIdType.MESH
T = 128
F32 = jnp.float32
NSEM = 128


def kernel(
    act, wt, rows, cols, gout,
    y_out, dx_out, dw_out,
    xall, gall, xst, gst, tiles, wd, dwd, dwt,
    dpart, dra, drb, drc, drd, dsum, dmine, zrecv,
    ypart, pair, ya, yb, yc, yd,
    ss, rs, ls, zss, zrs,
):
    r, c, d = lax.axis_index("row"), lax.axis_index("col"), lax.axis_index("depth")
    x, k, y, zl = r // 2, r % 2, c % 4, c // 4
    z = d * 4 + zl
    od = 1 - d

    def dev(dx=0, dk=0, dy=0, dz=0):
        zz = (z + dz + 8) % 8
        return {
            "row": ((x + dx + 4) % 4) * 2 + (k + dk) % 2,
            "col": (zz % 4) * 4 + (y + dy + 4) % 4,
            "depth": zz // 4,
        }

    def xs(zz, yy, lo=0, n=64):
        return xall.at[pl.ds(pl.multiple_of((zz * 4 + yy) * 64 + lo, 32), n)]

    def gs(dd, xx, kk, lo=0, n=128):
        return gall.at[pl.ds(pl.multiple_of(dd * 1024 + (xx * 2 + kk) * 128 + lo, 64), n)]

    zm = [(z + j + 8) % 8 for j in range(-4, 5)]
    zat = lambda j: zm[j + 4]
    yat = lambda j: (y + j + 4) % 4
    xat = lambda j: (x + j + 4) % 4

    ids = {}
    sent = {}

    def sem(name):
        if name not in ids:
            ids[name] = len(ids)
        return ids[name]

    def desc(name, src, dst, device):
        i = sem(name)
        return pltpu.make_async_remote_copy(
            src, dst, ss.at[i], rs.at[i], device_id=device, device_id_type=MESH
        )

    def send(name, make):
        desc(name, *make()).start()
        sent.setdefault(name, make)

    def recv(name, ref):
        desc(name, ref, ref, dev(dk=1)).wait_recv()

    local = [
        pltpu.make_async_copy(act.at[0], xs(z, y), ls.at[0]),
        pltpu.make_async_copy(gout.at[0], gs(d, x, k), ls.at[1]),
        pltpu.make_async_copy(wt.at[0, 0], tiles.at[pl.ds(0, 56)], ls.at[2]),
    ]
    for cp in local:
        cp.start()

    barrier = pltpu.get_barrier_semaphore()
    peers = [dev(dx=1), dev(dx=-1), dev(dk=1), dev(dy=1), dev(dy=-1)]
    peers += [dev(dz=j) for j in range(1, 8)]
    for peer in peers:
        pl.semaphore_signal(barrier, inc=1, device_id=peer, device_id_type=MESH)
    pl.semaphore_wait(barrier, len(peers))

    def z_send(h):
        if h < 3:
            up, down = zat(-h), zat(h)
            send(f"zu{h}", lambda: (act.at[0] if h == 0 else xs(up, y), xs(up, y), dev(dz=1)))
            send(f"zd{h}", lambda: (act.at[0] if h == 0 else xs(down, y), xs(down, y), dev(dz=-1)))
        else:
            send("zu3", lambda: (xs(zat(-3), y, 0, 32), xs(zat(-3), y, 0, 32), dev(dz=1)))
            send("zd3", lambda: (xs(zat(3), y, 32, 32), xs(zat(3), y, 32, 32), dev(dz=-1)))

    def z_recv(h):
        if h < 4:
            recv(f"zu{h - 1}", xs(zat(-h), y))
            recv(f"zd{h - 1}", xs(zat(h), y))
        else:
            recv("zu3", xs(zat(4), y, 0, 32))
            recv("zd3", xs(zat(4), y, 32, 32))

    def y_send(j, src=None):
        zz = zat(j)
        send(f"yu{j}", lambda: (xs(zz, y) if src is None else src, xs(zz, y), dev(dy=1)))
        send(f"yd{j}", lambda: (xs(zz, y) if src is None else src, xs(zz, y), dev(dy=-1)))

    def y_forward(j):
        zz = zat(j)
        recv(f"yu{j}", xs(zz, yat(-1)))
        send(f"yU{j}", lambda: (xs(zz, yat(-1), 0, 32), xs(zz, yat(-1), 0, 32), dev(dy=1)))
        recv(f"yd{j}", xs(zz, yat(1)))
        send(f"yD{j}", lambda: (xs(zz, yat(1), 32, 32), xs(zz, yat(1), 32, 32), dev(dy=-1)))

    def y_last(j):
        zz = zat(j)
        recv(f"yU{j}", xs(zz, yat(2), 0, 32))
        recv(f"yD{j}", xs(zz, yat(2), 32, 32))

    def both(h, own, do):
        up, down = zl + h < 4, zl - h >= 0
        if not own:
            up, down = jnp.logical_not(up), jnp.logical_not(down)
        pl.when(up)(lambda: do(h))
        pl.when(down)(lambda: do(-h))

    def g_send(tag, dd, src):
        send(f"gk0{tag}", lambda: (src, gs(dd, x, k), dev(dk=1)))
        send(f"gu{tag}", lambda: (src, gs(dd, x, k), dev(dx=1)))
        send(f"gd{tag}", lambda: (src, gs(dd, x, k), dev(dx=-1)))

    def g_forward(tag, dd):
        left, right = xat(-1), xat(1)
        recv(f"gu{tag}", gs(dd, left, k))
        send(f"gU{tag}", lambda: (gs(dd, left, k, 0, 64), gs(dd, left, k, 0, 64), dev(dx=1)))
        send(f"gk1{tag}", lambda: (gs(dd, left, k), gs(dd, left, k), dev(dk=1)))
        recv(f"gd{tag}", gs(dd, right, k))
        send(f"gD{tag}", lambda: (gs(dd, right, k, 64, 64), gs(dd, right, k, 64, 64), dev(dx=-1)))
        send(f"gk3{tag}", lambda: (gs(dd, right, k), gs(dd, right, k), dev(dk=1)))

    def g_last(tag, dd):
        far = xat(2)
        recv(f"gU{tag}", gs(dd, far, k, 0, 64))
        recv(f"gD{tag}", gs(dd, far, k, 64, 64))
        send(f"gk2{tag}", lambda: (gs(dd, far, k), gs(dd, far, k), dev(dk=1)))

    def g_core(tag, dd, j):
        xx = {0: x, 1: xat(-1), 2: xat(2), 3: xat(1)}[j]
        recv(f"gk{j}{tag}", gs(dd, xx, 1 - k))

    def g_stage(j):
        base = pl.multiple_of(d * 1024 + xat(j) * 256, 256)
        return pltpu.make_async_copy(gall.at[pl.ds(base, 256)], gst[j % 4], ls.at[8 + j % 4])

    def dx_compute(j):
        g_stage(j).start()
        g_stage(j).wait()

        @pl.loop(0, 4)
        def _(n):
            cut = pl.ds(pl.multiple_of(n * 256, 256), 256)
            dpart[j % 4][:, cut] = lax.dot_general(
                gst[j % 4][...], wd[cut, :],
                (((1,), (1,)), ((), ())), preferred_element_type=F32,
            )

    def dblock(q, j, half):
        return dpart[q % 4].at[pl.ds(pl.multiple_of(yat(j) * 64, 64), 64), pl.ds(half * 512, 512)]

    def dx_send(j):
        p = xat(j)
        send(f"da{j}", lambda: (dblock(j, 2, 0), dra[j % 4], dev(dy=1)))
        send(f"db{j}", lambda: (dblock(j, 2, 1), drb[j % 4], dev(dy=-1)))
        send(f"dc1{j}", lambda: (dblock(j, 1, 1), drc[j % 4][1], dev(dy=1)))
        send(f"dd0{j}", lambda: (dblock(j, -1, 0), drd[j % 4][0], dev(dy=-1)))

    def dx_middle(j):
        p = xat(j)
        recv(f"da{j}", dra[j % 4])
        dra[j % 4][...] += dblock(j, 1, 0)[...]
        send(f"dc0{j}", lambda: (dra[j % 4], drc[j % 4][0], dev(dy=1)))
        recv(f"db{j}", drb[j % 4])
        drb[j % 4][...] += dblock(j, -1, 1)[...]
        send(f"dd1{j}", lambda: (drb[j % 4], drd[j % 4][1], dev(dy=-1)))

    def dx_last(j):
        p = xat(j)
        for half in (1, 0):
            recv(f"dc{half}{j}", drc[j % 4][half])
            recv(f"dd{1 - half}{j}", drd[j % 4][1 - half])
        for half in range(2):
            dsum[j % 4][:, half * 512:half * 512 + 512] = (
                dblock(j, 0, half)[...] + drc[j % 4][half][...] + drd[j % 4][half][...]
            )

        @pl.when(p == zl)
        def _():
            dmine[...] = dsum[j % 4][...]

        @pl.when(p != zl)
        def _():
            slot = (zl - p + 4) % 4 - 1
            pltpu.make_async_remote_copy(
                dsum[j % 4], zrecv.at[slot], zss.at[slot], zrs.at[slot],
                device_id={"row": r, "col": p * 4 + y, "depth": d}, device_id_type=MESH,
            ).start()

    def x_stage(j):
        base = pl.multiple_of(d * 1024 + xat(j) * 256, 256)
        return pltpu.make_async_copy(xall.at[pl.ds(base, 256)], xst[j % 4], ls.at[4 + j % 4])

    def y_compute(j):
        x_stage(j).wait()

        @pl.loop(0, 7)
        def _(n):
            cut = pl.ds(pl.multiple_of(n * 256, 256), 256)
            ypart[j % 4][:, cut] = jnp.dot(
                xst[j % 4][...], wd[:, cut], preferred_element_type=F32
            )

        send(f"p{j}", lambda: (ypart[j % 4].at[pl.ds(pl.multiple_of((1 - k) * 128, 128), 128)], pair[j % 4], dev(dk=1)))

    def yblock(j, half):
        return pair[j % 4].at[:, pl.ds(half * 896, 896)]

    def y_pair(j):
        recv(f"p{j}", pair[j % 4])
        pair[j % 4][...] += ypart[j % 4][pl.ds(pl.multiple_of(k * 128, 128), 128), :]

    local[2].wait()
    tiles[56] = jnp.zeros((T, T), jnp.bfloat16)

    g_send("o", d, gout.at[0])
    z_send(0)
    y_send(0, act.at[0])

    def fill(i, at):
        for j in range(14):
            cell = i * 14 + j
            here = jnp.minimum(at, 55)
            hit = jnp.logical_and(at < 56, rows[0, 0, here] * 14 + cols[0, 0, here] == cell)
            wd[pl.ds(pl.multiple_of(i * T, T), T), j * T:j * T + T] = tiles[jnp.where(hit, at, 56)]
            at = at + hit.astype(jnp.int32)
        return at

    lax.fori_loop(0, 8, fill, jnp.int32(0))

    def dw_compute(dd, first):
        base = pl.multiple_of(dd * 1024, 1024)

        @pl.loop(0, 7)
        def _(n):
            cut = pl.ds(pl.multiple_of(n * 256, 256), 256)
            got = lax.dot_general(
                xall[pl.ds(base, 1024), :], gall[pl.ds(base, 1024), cut],
                (((0,), (0,)), ((), ())), preferred_element_type=F32,
            )
            for i in range(8):
                for j in range(2):
                    part = got[i * T:i * T + T, j * T:j * T + T]
                    at = i * 14 + n * 2 + j
                    dwd[at] = part if first else dwd[at] + part

    def out_send():
        send("oa", lambda: (yblock(2, 0), ya, dev(dx=1)))
        send("ob", lambda: (yblock(2, 1), yb, dev(dx=-1)))

    def out_middle():
        recv("oa", ya)
        ya[...] += yblock(1, 0)[...]
        send("oc0", lambda: (ya, yc[0], dev(dx=1)))
        recv("ob", yb)
        yb[...] += yblock(-1, 1)[...]
        send("od1", lambda: (yb, yd[1], dev(dx=-1)))

    z_recv(1)
    z_send(1)
    both(1, True, y_send)
    y_forward(0)
    local[1].wait()
    g_core("o", d, 0)
    dx_compute(0)
    z_recv(2)
    z_send(2)
    both(2, True, y_send)
    both(1, True, y_forward)
    z_recv(3)
    z_send(3)
    both(3, True, y_send)
    dx_send(0)
    send("gz0", lambda: (gout.at[0, pl.ds(0, 64)], gs(d, x, k, 0, 64), dev(dz=4)))
    send("gz1", lambda: (gout.at[0, pl.ds(64, 64)], gs(d, x, k, 64, 64), dev(dz=4)))
    both(2, True, y_forward)
    g_forward("o", d)
    g_core("o", d, 1)
    dx_compute(-1)
    g_core("o", d, 3)
    dx_compute(1)
    both(3, True, y_forward)
    dx_middle(0)
    dx_send(-1)
    dx_send(1)
    local[0].wait()
    y_last(0)
    for h in (1, 2, 3):
        both(h, True, y_last)
    for j in (2, 1, -1, 0):
        x_stage(j).start()
    y_compute(2)
    y_compute(1)
    y_pair(2)
    out_send()
    y_compute(-1)
    y_pair(1)
    send("oc1", lambda: (yblock(1, 1), yc[1], dev(dx=1)))
    y_pair(-1)
    send("od0", lambda: (yblock(-1, 0), yd[0], dev(dx=-1)))
    g_last("o", d)
    g_core("o", d, 2)
    dx_compute(2)
    dx_send(2)
    z_recv(4)
    for h in (1, 2, 3):
        both(h, False, y_send)
    y_send(4)
    y_compute(0)
    recv("gz0", gs(od, x, k, 0, 64))
    recv("gz1", gs(od, x, k, 64, 64))
    g_send("t", od, gs(od, x, k))
    dx_middle(-1)
    dx_middle(1)
    dw_compute(d, True)
    for h in (1, 2, 3):
        both(h, False, y_forward)
    y_forward(4)
    dx_middle(2)
    dx_last(0)
    dx_last(-1)
    dx_last(1)
    out_middle()
    g_forward("t", od)
    dx_last(2)
    for h in (1, 2, 3):
        both(h, False, y_last)
    y_last(4)
    y_pair(0)
    g_last("t", od)
    for j in range(4):
        g_core("t", od, j)
    dw_compute(od, False)

    scale = 1.0 / math.sqrt(2048.0)

    @pl.loop(0, 8)
    def _(n):
        for i in range(7):
            t = n * 7 + i
            dwt[t] = dwd[rows[0, 0, t] * 14 + cols[0, 0, t]] * scale

    out = pltpu.make_async_copy(dwt, dw_out.at[0, 0], ls.at[3])
    out.start()
    for half in range(2):
        recv(f"oc{1 - half}", yc[1 - half])
        recv(f"od{half}", yd[half])
    for half in range(2):
        y_out[0, :, half * 896:half * 896 + 896] = (
            yblock(0, half)[...] + yc[half][...] + yd[half][...]
        ).astype(jnp.bfloat16)
    for slot in range(3):
        pltpu.make_async_remote_copy(
            zrecv.at[slot], zrecv.at[slot], zss.at[slot], zrs.at[slot],
            device_id=dev(dk=1), device_id_type=MESH,
        ).wait()
    dx_out[0] = (dmine[...] + zrecv[0] + zrecv[1] + zrecv[2]).astype(jnp.bfloat16)
    out.wait()
    for name, make in sent.items():
        desc(name, *make()).wait_send()


def hand_over(y_in, dx_in, dw_in, y_out, dx_out, dw_out, y_mid, dx_mid, dw_mid, sem):
    steps = [(y_in, y_mid, y_out), (dx_in, dx_mid, dx_out)]
    for i in range(4):
        cut = pl.ds(i * 14, 14)
        steps.append((dw_in.at[0, 0, cut], dw_mid.at[cut], dw_out.at[0, 0, cut]))
    into = [pltpu.make_async_copy(a, b, sem.at[0, i]) for i, (a, b, c) in enumerate(steps)]
    out = [pltpu.make_async_copy(b, c, sem.at[1, i]) for i, (a, b, c) in enumerate(steps)]
    for cp in into:
        cp.start()
    for first, second in zip(into, out):
        first.wait()
        second.start()
    for cp in out:
        cp.wait()


def shards(act, wt, rows, cols, gout):
    hbm = pl.BlockSpec(memory_space=pl.ANY)
    smem = pl.BlockSpec(memory_space=pltpu.SMEM)
    vmem = pl.BlockSpec(memory_space=pltpu.VMEM)
    bf16 = jnp.bfloat16
    dma = pltpu.SemaphoreType.DMA
    outs = [
        jax.ShapeDtypeStruct((1, 128, 1792), bf16),
        jax.ShapeDtypeStruct((1, 64, 1024), bf16),
        jax.ShapeDtypeStruct((1, 1, 56, T, T), F32),
    ]
    results = tuple(
        pl.pallas_call(
            kernel,
            out_shape=outs,
            in_specs=[hbm, hbm, smem, smem, hbm],
            out_specs=[vmem, vmem, hbm],
            scratch_shapes=[
                pltpu.VMEM((2048, 1024), bf16),
                pltpu.VMEM((2048, 1792), bf16),
                [pltpu.VMEM((256, 1024), bf16)] * 4,
                [pltpu.VMEM((256, 1792), bf16)] * 4,
                pltpu.VMEM((57, T, T), bf16),
                pltpu.VMEM((1024, 1792), bf16),
                pltpu.VMEM((112, T, T), F32),
                pltpu.VMEM((56, T, T), F32),
                [pltpu.VMEM((256, 1024), F32)] * 4,
                [pltpu.VMEM((64, 512), F32)] * 4,
                [pltpu.VMEM((64, 512), F32)] * 4,
                [[pltpu.VMEM((64, 512), F32)] * 2] * 4,
                [[pltpu.VMEM((64, 512), F32)] * 2] * 4,
                [pltpu.VMEM((64, 1024), F32)] * 4,
                pltpu.VMEM((64, 1024), F32),
                pltpu.VMEM((3, 64, 1024), F32),
                [pltpu.VMEM((256, 1792), F32)] * 4,
                [pltpu.VMEM((128, 1792), F32)] * 4,
                pltpu.VMEM((128, 896), F32),
                pltpu.VMEM((128, 896), F32),
                [pltpu.VMEM((128, 896), F32)] * 2,
                [pltpu.VMEM((128, 896), F32)] * 2,
                dma((NSEM,)), dma((NSEM,)), dma((12,)), dma((3,)), dma((3,)),
            ],
            compiler_params=pltpu.CompilerParams(
                collective_id=0, has_side_effects=True, vmem_limit_bytes=62 * 2**20
            ),
        )(act, wt, rows, cols, gout)
    )
    return tuple(
        pl.pallas_call(
            hand_over,
            out_shape=outs,
            in_specs=[hbm] * 3,
            out_specs=[hbm] * 3,
            scratch_shapes=[
                pltpu.VMEM((1, 128, 1792), bf16),
                pltpu.VMEM((1, 64, 1024), bf16),
                pltpu.VMEM((56, T, T), F32),
                dma((2, 6)),
            ],
            compiler_params=pltpu.CompilerParams(vmem_limit_bytes=60 * 2**20),
        )(*results)
    )


def solution(mesh):
    placed = (
        P("depth", "col", "row"),
        P("row", "col", None, None, None),
        P("row", "col", None),
        P("row", "col", None),
        P("depth", "row", "col"),
    )
    return jax.shard_map(
        shards,
        mesh=mesh,
        in_specs=placed,
        out_specs=(
            P("depth", "row", "col"),
            P("depth", "col", "row"),
            P("row", "col", None, None, None),
        ),
        check_vma=False,
    )
```

```python
import functools
import math

import jax
import jax.numpy as jnp
from jax import lax
from jax.experimental import pallas as pl
from jax.experimental.pallas import tpu as pltpu
from jax.sharding import PartitionSpec as P

MESH = pl.DeviceIdType.MESH
T = 128
F32 = jnp.float32
NSEM = 128


def kernel(
    act, wt, rows, cols, gout,
    y_out, dx_out, dw_out,
    xall, gall, xst, gst, tiles, wd, dwd, dwt,
    dpart, dra, drb, drc, drd, dsum, dmine, zrecv,
    ypart, pair, ya, yb, yc, yd,
    ss, rs, ls, zss, zrs,
):
    r, c, d = lax.axis_index("row"), lax.axis_index("col"), lax.axis_index("depth")
    x, k, y, zl = r // 2, r % 2, c % 4, c // 4
    z = d * 4 + zl
    od = 1 - d

    def dev(dx=0, dk=0, dy=0, dz=0):
        zz = (z + dz + 8) % 8
        return {
            "row": ((x + dx + 4) % 4) * 2 + (k + dk) % 2,
            "col": (zz % 4) * 4 + (y + dy + 4) % 4,
            "depth": zz // 4,
        }

    def xs(zz, yy, lo=0, n=64):
        return xall.at[pl.ds(pl.multiple_of((zz * 4 + yy) * 64 + lo, 32), n)]

    def gs(dd, xx, kk, lo=0, n=128):
        return gall.at[pl.ds(pl.multiple_of(dd * 1024 + (xx * 2 + kk) * 128 + lo, 64), n)]

    zm = [(z + j + 8) % 8 for j in range(-4, 5)]
    zat = lambda j: zm[j + 4]
    yat = lambda j: (y + j + 4) % 4
    xat = lambda j: (x + j + 4) % 4

    ids = {}
    sent = {}

    def sem(name):
        if name not in ids:
            ids[name] = len(ids)
        return ids[name]

    def desc(name, src, dst, device):
        i = sem(name)
        return pltpu.make_async_remote_copy(
            src, dst, ss.at[i], rs.at[i], device_id=device, device_id_type=MESH
        )

    def send(name, make):
        desc(name, *make()).start()
        sent.setdefault(name, make)

    def recv(name, ref):
        desc(name, ref, ref, dev(dk=1)).wait_recv()

    local = [
        pltpu.make_async_copy(act.at[0], xs(z, y), ls.at[0]),
        pltpu.make_async_copy(gout.at[0], gs(d, x, k), ls.at[1]),
        pltpu.make_async_copy(wt.at[0, 0], tiles.at[pl.ds(0, 56)], ls.at[2]),
    ]
    for cp in local:
        cp.start()

    barrier = pltpu.get_barrier_semaphore()
    peers = [dev(dx=1), dev(dx=-1), dev(dk=1), dev(dy=1), dev(dy=-1)]
    peers += [dev(dz=j) for j in range(1, 8)]
    for peer in peers:
        pl.semaphore_signal(barrier, inc=1, device_id=peer, device_id_type=MESH)
    pl.semaphore_wait(barrier, len(peers))

    def z_send(h):
        if h < 3:
            up, down = zat(-h), zat(h)
            send(f"zu{h}", lambda: (act.at[0] if h == 0 else xs(up, y), xs(up, y), dev(dz=1)))
            send(f"zd{h}", lambda: (act.at[0] if h == 0 else xs(down, y), xs(down, y), dev(dz=-1)))
        else:
            send("zu3", lambda: (xs(zat(-3), y, 0, 32), xs(zat(-3), y, 0, 32), dev(dz=1)))
            send("zd3", lambda: (xs(zat(3), y, 32, 32), xs(zat(3), y, 32, 32), dev(dz=-1)))

    def z_recv(h):
        if h < 4:
            recv(f"zu{h - 1}", xs(zat(-h), y))
            recv(f"zd{h - 1}", xs(zat(h), y))
        else:
            recv("zu3", xs(zat(4), y, 0, 32))
            recv("zd3", xs(zat(4), y, 32, 32))

    def y_send(j, src=None):
        zz = zat(j)
        send(f"yu{j}", lambda: (xs(zz, y) if src is None else src, xs(zz, y), dev(dy=1)))
        send(f"yd{j}", lambda: (xs(zz, y) if src is None else src, xs(zz, y), dev(dy=-1)))

    def y_forward(j):
        zz = zat(j)
        recv(f"yu{j}", xs(zz, yat(-1)))
        send(f"yU{j}", lambda: (xs(zz, yat(-1), 0, 32), xs(zz, yat(-1), 0, 32), dev(dy=1)))
        recv(f"yd{j}", xs(zz, yat(1)))
        send(f"yD{j}", lambda: (xs(zz, yat(1), 32, 32), xs(zz, yat(1), 32, 32), dev(dy=-1)))

    def y_last(j):
        zz = zat(j)
        recv(f"yU{j}", xs(zz, yat(2), 0, 32))
        recv(f"yD{j}", xs(zz, yat(2), 32, 32))

    def both(h, own, do):
        up, down = zl + h < 4, zl - h >= 0
        if not own:
            up, down = jnp.logical_not(up), jnp.logical_not(down)
        pl.when(up)(lambda: do(h))
        pl.when(down)(lambda: do(-h))

    def g_send(tag, dd, src):
        send(f"gk0{tag}", lambda: (src, gs(dd, x, k), dev(dk=1)))
        send(f"gu{tag}", lambda: (src, gs(dd, x, k), dev(dx=1)))
        send(f"gd{tag}", lambda: (src, gs(dd, x, k), dev(dx=-1)))

    def g_forward(tag, dd):
        left, right = xat(-1), xat(1)
        recv(f"gu{tag}", gs(dd, left, k))
        send(f"gU{tag}", lambda: (gs(dd, left, k, 0, 64), gs(dd, left, k, 0, 64), dev(dx=1)))
        send(f"gk1{tag}", lambda: (gs(dd, left, k), gs(dd, left, k), dev(dk=1)))
        recv(f"gd{tag}", gs(dd, right, k))
        send(f"gD{tag}", lambda: (gs(dd, right, k, 64, 64), gs(dd, right, k, 64, 64), dev(dx=-1)))
        send(f"gk3{tag}", lambda: (gs(dd, right, k), gs(dd, right, k), dev(dk=1)))

    def g_last(tag, dd):
        far = xat(2)
        recv(f"gU{tag}", gs(dd, far, k, 0, 64))
        recv(f"gD{tag}", gs(dd, far, k, 64, 64))
        send(f"gk2{tag}", lambda: (gs(dd, far, k), gs(dd, far, k), dev(dk=1)))

    def g_core(tag, dd, j):
        xx = {0: x, 1: xat(-1), 2: xat(2), 3: xat(1)}[j]
        recv(f"gk{j}{tag}", gs(dd, xx, 1 - k))

    def g_stage(j):
        base = pl.multiple_of(d * 1024 + xat(j) * 256, 256)
        return pltpu.make_async_copy(gall.at[pl.ds(base, 256)], gst[j % 4], ls.at[8 + j % 4])

    def dx_compute(j):
        g_stage(j).start()
        g_stage(j).wait()

        @pl.loop(0, 4)
        def _(n):
            cut = pl.ds(pl.multiple_of(n * 256, 256), 256)
            dpart[j % 4][:, cut] = lax.dot_general(
                gst[j % 4][...], wd[cut, :],
                (((1,), (1,)), ((), ())), preferred_element_type=F32,
            )

    def dblock(q, j, half):
        return dpart[q % 4].at[pl.ds(pl.multiple_of(yat(j) * 64, 64), 64), pl.ds(half * 512, 512)]

    def dx_send(j):
        p = xat(j)
        send(f"da{j}", lambda: (dblock(j, 2, 0), dra[j % 4], dev(dy=1)))
        send(f"db{j}", lambda: (dblock(j, 2, 1), drb[j % 4], dev(dy=-1)))
        send(f"dc1{j}", lambda: (dblock(j, 1, 1), drc[j % 4][1], dev(dy=1)))
        send(f"dd0{j}", lambda: (dblock(j, -1, 0), drd[j % 4][0], dev(dy=-1)))

    def dx_middle(j):
        p = xat(j)
        recv(f"da{j}", dra[j % 4])
        dra[j % 4][...] += dblock(j, 1, 0)[...]
        send(f"dc0{j}", lambda: (dra[j % 4], drc[j % 4][0], dev(dy=1)))
        recv(f"db{j}", drb[j % 4])
        drb[j % 4][...] += dblock(j, -1, 1)[...]
        send(f"dd1{j}", lambda: (drb[j % 4], drd[j % 4][1], dev(dy=-1)))

    def dx_last(j):
        p = xat(j)
        for half in (1, 0):
            recv(f"dc{half}{j}", drc[j % 4][half])
            recv(f"dd{1 - half}{j}", drd[j % 4][1 - half])
        for half in range(2):
            dsum[j % 4][:, half * 512:half * 512 + 512] = (
                dblock(j, 0, half)[...] + drc[j % 4][half][...] + drd[j % 4][half][...]
            )

        @pl.when(p == zl)
        def _():
            dmine[...] = dsum[j % 4][...]

        @pl.when(p != zl)
        def _():
            slot = (zl - p + 4) % 4 - 1
            pltpu.make_async_remote_copy(
                dsum[j % 4], zrecv.at[slot], zss.at[slot], zrs.at[slot],
                device_id={"row": r, "col": p * 4 + y, "depth": d}, device_id_type=MESH,
            ).start()

    def x_stage(j):
        base = pl.multiple_of(d * 1024 + xat(j) * 256, 256)
        return pltpu.make_async_copy(xall.at[pl.ds(base, 256)], xst[j % 4], ls.at[4 + j % 4])

    def y_compute(j):
        x_stage(j).wait()

        @pl.loop(0, 7)
        def _(n):
            cut = pl.ds(pl.multiple_of(n * 256, 256), 256)
            ypart[j % 4][:, cut] = jnp.dot(
                xst[j % 4][...], wd[:, cut], preferred_element_type=F32
            )

        send(f"p{j}", lambda: (ypart[j % 4].at[pl.ds(pl.multiple_of((1 - k) * 128, 128), 128)], pair[j % 4], dev(dk=1)))

    def yblock(j, half):
        return pair[j % 4].at[:, pl.ds(half * 896, 896)]

    def y_pair(j):
        recv(f"p{j}", pair[j % 4])
        pair[j % 4][...] += ypart[j % 4][pl.ds(pl.multiple_of(k * 128, 128), 128), :]

    local[2].wait()
    tiles[56] = jnp.zeros((T, T), jnp.bfloat16)

    g_send("o", d, gout.at[0])
    z_send(0)
    y_send(0, act.at[0])

    def fill(i, at):
        for j in range(14):
            cell = i * 14 + j
            here = jnp.minimum(at, 55)
            hit = jnp.logical_and(at < 56, rows[0, 0, here] * 14 + cols[0, 0, here] == cell)
            wd[pl.ds(pl.multiple_of(i * T, T), T), j * T:j * T + T] = tiles[jnp.where(hit, at, 56)]
            at = at + hit.astype(jnp.int32)
        return at

    lax.fori_loop(0, 8, fill, jnp.int32(0))

    def dw_compute(dd, first):
        base = pl.multiple_of(dd * 1024, 1024)

        @pl.loop(0, 7)
        def _(n):
            cut = pl.ds(pl.multiple_of(n * 256, 256), 256)
            got = lax.dot_general(
                xall[pl.ds(base, 1024), :], gall[pl.ds(base, 1024), cut],
                (((0,), (0,)), ((), ())), preferred_element_type=F32,
            )
            for i in range(8):
                for j in range(2):
                    part = got[i * T:i * T + T, j * T:j * T + T]
                    at = i * 14 + n * 2 + j
                    dwd[at] = part if first else dwd[at] + part

    def out_send():
        send("oa", lambda: (yblock(2, 0), ya, dev(dx=1)))
        send("ob", lambda: (yblock(2, 1), yb, dev(dx=-1)))

    def out_middle():
        recv("oa", ya)
        ya[...] += yblock(1, 0)[...]
        send("oc0", lambda: (ya, yc[0], dev(dx=1)))
        recv("ob", yb)
        yb[...] += yblock(-1, 1)[...]
        send("od1", lambda: (yb, yd[1], dev(dx=-1)))

    z_recv(1)
    z_send(1)
    both(1, True, y_send)
    y_forward(0)
    local[1].wait()
    g_core("o", d, 0)
    dx_compute(0)
    z_recv(2)
    z_send(2)
    both(2, True, y_send)
    both(1, True, y_forward)
    z_recv(3)
    z_send(3)
    both(3, True, y_send)
    dx_send(0)
    send("gz0", lambda: (gout.at[0, pl.ds(0, 64)], gs(d, x, k, 0, 64), dev(dz=4)))
    send("gz1", lambda: (gout.at[0, pl.ds(64, 64)], gs(d, x, k, 64, 64), dev(dz=4)))
    both(2, True, y_forward)
    g_forward("o", d)
    g_core("o", d, 1)
    dx_compute(-1)
    g_core("o", d, 3)
    dx_compute(1)
    both(3, True, y_forward)
    dx_middle(0)
    dx_send(-1)
    dx_send(1)
    local[0].wait()
    y_last(0)
    for h in (1, 2, 3):
        both(h, True, y_last)
    for j in (2, 1, -1, 0):
        x_stage(j).start()
    y_compute(2)
    y_compute(1)
    y_pair(2)
    out_send()
    y_compute(-1)
    y_pair(1)
    send("oc1", lambda: (yblock(1, 1), yc[1], dev(dx=1)))
    y_pair(-1)
    send("od0", lambda: (yblock(-1, 0), yd[0], dev(dx=-1)))
    g_last("o", d)
    g_core("o", d, 2)
    dx_compute(2)
    dx_send(2)
    z_recv(4)
    for h in (1, 2, 3):
        both(h, False, y_send)
    y_send(4)
    y_compute(0)
    recv("gz0", gs(od, x, k, 0, 64))
    recv("gz1", gs(od, x, k, 64, 64))
    g_send("t", od, gs(od, x, k))
    dx_middle(-1)
    dx_middle(1)
    dw_compute(d, True)
    out_middle()
    for h in (1, 2, 3):
        both(h, False, y_forward)
    y_forward(4)
    dx_middle(2)
    g_forward("t", od)
    dx_last(0)
    dx_last(-1)
    dx_last(1)
    dx_last(2)
    for h in (1, 2, 3):
        both(h, False, y_last)
    y_last(4)
    y_pair(0)
    g_last("t", od)
    for j in range(4):
        g_core("t", od, j)
    dw_compute(od, False)

    scale = 1.0 / math.sqrt(2048.0)

    @pl.loop(0, 8)
    def _(n):
        for i in range(7):
            t = n * 7 + i
            dwt[t] = dwd[rows[0, 0, t] * 14 + cols[0, 0, t]] * scale

    out = pltpu.make_async_copy(dwt, dw_out.at[0, 0], ls.at[3])
    out.start()
    for half in range(2):
        recv(f"oc{1 - half}", yc[1 - half])
        recv(f"od{half}", yd[half])
    for half in range(2):
        y_out[0, :, half * 896:half * 896 + 896] = (
            yblock(0, half)[...] + yc[half][...] + yd[half][...]
        ).astype(jnp.bfloat16)
    for slot in range(3):
        pltpu.make_async_remote_copy(
            zrecv.at[slot], zrecv.at[slot], zss.at[slot], zrs.at[slot],
            device_id=dev(dk=1), device_id_type=MESH,
        ).wait()
    dx_out[0] = (dmine[...] + zrecv[0] + zrecv[1] + zrecv[2]).astype(jnp.bfloat16)
    out.wait()
    for name, make in sent.items():
        desc(name, *make()).wait_send()


def hand_over(y_in, dx_in, dw_in, y_out, dx_out, dw_out, y_mid, dx_mid, dw_mid, sem):
    steps = [(y_in, y_mid, y_out), (dx_in, dx_mid, dx_out)]
    for i in range(4):
        cut = pl.ds(i * 14, 14)
        steps.append((dw_in.at[0, 0, cut], dw_mid.at[cut], dw_out.at[0, 0, cut]))
    into = [pltpu.make_async_copy(a, b, sem.at[0, i]) for i, (a, b, c) in enumerate(steps)]
    out = [pltpu.make_async_copy(b, c, sem.at[1, i]) for i, (a, b, c) in enumerate(steps)]
    for cp in into:
        cp.start()
    for first, second in zip(into, out):
        first.wait()
        second.start()
    for cp in out:
        cp.wait()


def shards(act, wt, rows, cols, gout):
    hbm = pl.BlockSpec(memory_space=pl.ANY)
    smem = pl.BlockSpec(memory_space=pltpu.SMEM)
    vmem = pl.BlockSpec(memory_space=pltpu.VMEM)
    bf16 = jnp.bfloat16
    dma = pltpu.SemaphoreType.DMA
    outs = [
        jax.ShapeDtypeStruct((1, 128, 1792), bf16),
        jax.ShapeDtypeStruct((1, 64, 1024), bf16),
        jax.ShapeDtypeStruct((1, 1, 56, T, T), F32),
    ]
    results = tuple(
        pl.pallas_call(
            kernel,
            out_shape=outs,
            in_specs=[hbm, hbm, smem, smem, hbm],
            out_specs=[vmem, vmem, hbm],
            scratch_shapes=[
                pltpu.VMEM((2048, 1024), bf16),
                pltpu.VMEM((2048, 1792), bf16),
                [pltpu.VMEM((256, 1024), bf16)] * 4,
                [pltpu.VMEM((256, 1792), bf16)] * 4,
                pltpu.VMEM((57, T, T), bf16),
                pltpu.VMEM((1024, 1792), bf16),
                pltpu.VMEM((112, T, T), F32),
                pltpu.VMEM((56, T, T), F32),
                [pltpu.VMEM((256, 1024), F32)] * 4,
                [pltpu.VMEM((64, 512), F32)] * 4,
                [pltpu.VMEM((64, 512), F32)] * 4,
                [[pltpu.VMEM((64, 512), F32)] * 2] * 4,
                [[pltpu.VMEM((64, 512), F32)] * 2] * 4,
                [pltpu.VMEM((64, 1024), F32)] * 4,
                pltpu.VMEM((64, 1024), F32),
                pltpu.VMEM((3, 64, 1024), F32),
                [pltpu.VMEM((256, 1792), F32)] * 4,
                [pltpu.VMEM((128, 1792), F32)] * 4,
                pltpu.VMEM((128, 896), F32),
                pltpu.VMEM((128, 896), F32),
                [pltpu.VMEM((128, 896), F32)] * 2,
                [pltpu.VMEM((128, 896), F32)] * 2,
                dma((NSEM,)), dma((NSEM,)), dma((12,)), dma((3,)), dma((3,)),
            ],
            compiler_params=pltpu.CompilerParams(
                collective_id=0, has_side_effects=True, vmem_limit_bytes=62 * 2**20
            ),
        )(act, wt, rows, cols, gout)
    )
    return tuple(
        pl.pallas_call(
            hand_over,
            out_shape=outs,
            in_specs=[hbm] * 3,
            out_specs=[hbm] * 3,
            scratch_shapes=[
                pltpu.VMEM((1, 128, 1792), bf16),
                pltpu.VMEM((1, 64, 1024), bf16),
                pltpu.VMEM((56, T, T), F32),
                dma((2, 6)),
            ],
            compiler_params=pltpu.CompilerParams(vmem_limit_bytes=60 * 2**20),
        )(*results)
    )


def solution(mesh):
    placed = (
        P("depth", "col", "row"),
        P("row", "col", None, None, None),
        P("row", "col", None),
        P("row", "col", None),
        P("depth", "row", "col"),
    )
    return jax.shard_map(
        shards,
        mesh=mesh,
        in_specs=placed,
        out_specs=(
            P("depth", "row", "col"),
            P("depth", "col", "row"),
            P("row", "col", None, None, None),
        ),
        check_vma=False,
    )
```

```python
import functools
import math

import jax
import jax.numpy as jnp
from jax import lax
from jax.experimental import pallas as pl
from jax.experimental.pallas import tpu as pltpu
from jax.sharding import PartitionSpec as P

MESH = pl.DeviceIdType.MESH
T = 128
F32 = jnp.float32
NSEM = 128


def kernel(
    act, wt, rows, cols, gout,
    y_out, dx_out, dw_out,
    xall, gall, xst, gst, tiles, wd, dwd, dwt,
    dpart, dra, drb, drc, drd, dsum, dmine, zrecv,
    ypart, pair, ya, yb, yc, yd,
    ss, rs, ls, zss, zrs,
):
    r, c, d = lax.axis_index("row"), lax.axis_index("col"), lax.axis_index("depth")
    x, k, y, zl = r // 2, r % 2, c % 4, c // 4
    z = d * 4 + zl
    od = 1 - d

    def dev(dx=0, dk=0, dy=0, dz=0):
        zz = (z + dz + 8) % 8
        return {
            "row": ((x + dx + 4) % 4) * 2 + (k + dk) % 2,
            "col": (zz % 4) * 4 + (y + dy + 4) % 4,
            "depth": zz // 4,
        }

    def xs(zz, yy, lo=0, n=64):
        return xall.at[pl.ds(pl.multiple_of((zz * 4 + yy) * 64 + lo, 32), n)]

    def gs(dd, xx, kk, lo=0, n=128):
        return gall.at[pl.ds(pl.multiple_of(dd * 1024 + (xx * 2 + kk) * 128 + lo, 64), n)]

    zm = [(z + j + 8) % 8 for j in range(-4, 5)]
    zat = lambda j: zm[j + 4]
    yat = lambda j: (y + j + 4) % 4
    xat = lambda j: (x + j + 4) % 4

    ids = {}
    sent = {}

    def sem(name):
        if name not in ids:
            ids[name] = len(ids)
        return ids[name]

    def desc(name, src, dst, device):
        i = sem(name)
        return pltpu.make_async_remote_copy(
            src, dst, ss.at[i], rs.at[i], device_id=device, device_id_type=MESH
        )

    def send(name, make):
        desc(name, *make()).start()
        sent.setdefault(name, make)

    def recv(name, ref):
        desc(name, ref, ref, dev(dk=1)).wait_recv()

    local = [
        pltpu.make_async_copy(act.at[0], xs(z, y), ls.at[0]),
        pltpu.make_async_copy(gout.at[0], gs(d, x, k), ls.at[1]),
        pltpu.make_async_copy(wt.at[0, 0], tiles.at[pl.ds(0, 56)], ls.at[2]),
    ]
    for cp in local:
        cp.start()

    barrier = pltpu.get_barrier_semaphore()
    peers = [dev(dx=1), dev(dx=-1), dev(dk=1), dev(dy=1), dev(dy=-1)]
    peers += [dev(dz=j) for j in range(1, 8)]
    for peer in peers:
        pl.semaphore_signal(barrier, inc=1, device_id=peer, device_id_type=MESH)
    pl.semaphore_wait(barrier, len(peers))

    def z_send(h):
        if h < 3:
            up, down = zat(-h), zat(h)
            send(f"zu{h}", lambda: (act.at[0] if h == 0 else xs(up, y), xs(up, y), dev(dz=1)))
            send(f"zd{h}", lambda: (act.at[0] if h == 0 else xs(down, y), xs(down, y), dev(dz=-1)))
        else:
            send("zu3", lambda: (xs(zat(-3), y, 0, 32), xs(zat(-3), y, 0, 32), dev(dz=1)))
            send("zd3", lambda: (xs(zat(3), y, 32, 32), xs(zat(3), y, 32, 32), dev(dz=-1)))

    def z_recv(h):
        if h < 4:
            recv(f"zu{h - 1}", xs(zat(-h), y))
            recv(f"zd{h - 1}", xs(zat(h), y))
        else:
            recv("zu3", xs(zat(4), y, 0, 32))
            recv("zd3", xs(zat(4), y, 32, 32))

    def y_send(j, src=None):
        zz = zat(j)
        send(f"yu{j}", lambda: (xs(zz, y) if src is None else src, xs(zz, y), dev(dy=1)))
        send(f"yd{j}", lambda: (xs(zz, y) if src is None else src, xs(zz, y), dev(dy=-1)))

    def y_forward(j):
        zz = zat(j)
        recv(f"yu{j}", xs(zz, yat(-1)))
        send(f"yU{j}", lambda: (xs(zz, yat(-1), 0, 32), xs(zz, yat(-1), 0, 32), dev(dy=1)))
        recv(f"yd{j}", xs(zz, yat(1)))
        send(f"yD{j}", lambda: (xs(zz, yat(1), 32, 32), xs(zz, yat(1), 32, 32), dev(dy=-1)))

    def y_last(j):
        zz = zat(j)
        recv(f"yU{j}", xs(zz, yat(2), 0, 32))
        recv(f"yD{j}", xs(zz, yat(2), 32, 32))

    def both(h, own, do):
        up, down = zl + h < 4, zl - h >= 0
        if not own:
            up, down = jnp.logical_not(up), jnp.logical_not(down)
        pl.when(up)(lambda: do(h))
        pl.when(down)(lambda: do(-h))

    def g_send(tag, dd, src):
        send(f"gk0{tag}", lambda: (src, gs(dd, x, k), dev(dk=1)))
        send(f"gu{tag}", lambda: (src, gs(dd, x, k), dev(dx=1)))
        send(f"gd{tag}", lambda: (src, gs(dd, x, k), dev(dx=-1)))

    def g_forward(tag, dd):
        left, right = xat(-1), xat(1)
        recv(f"gu{tag}", gs(dd, left, k))
        send(f"gU{tag}", lambda: (gs(dd, left, k, 0, 64), gs(dd, left, k, 0, 64), dev(dx=1)))
        send(f"gk1{tag}", lambda: (gs(dd, left, k), gs(dd, left, k), dev(dk=1)))
        recv(f"gd{tag}", gs(dd, right, k))
        send(f"gD{tag}", lambda: (gs(dd, right, k, 64, 64), gs(dd, right, k, 64, 64), dev(dx=-1)))
        send(f"gk3{tag}", lambda: (gs(dd, right, k), gs(dd, right, k), dev(dk=1)))

    def g_last(tag, dd):
        far = xat(2)
        recv(f"gU{tag}", gs(dd, far, k, 0, 64))
        recv(f"gD{tag}", gs(dd, far, k, 64, 64))
        send(f"gk2{tag}", lambda: (gs(dd, far, k), gs(dd, far, k), dev(dk=1)))

    def g_core(tag, dd, j):
        xx = {0: x, 1: xat(-1), 2: xat(2), 3: xat(1)}[j]
        recv(f"gk{j}{tag}", gs(dd, xx, 1 - k))

    def g_stage(j):
        base = pl.multiple_of(d * 1024 + xat(j) * 256, 256)
        return pltpu.make_async_copy(gall.at[pl.ds(base, 256)], gst[j % 4], ls.at[8 + j % 4])

    def dx_compute(j):
        g_stage(j).start()
        g_stage(j).wait()

        @pl.loop(0, 4)
        def _(n):
            cut = pl.ds(pl.multiple_of(n * 256, 256), 256)
            dpart[j % 4][:, cut] = lax.dot_general(
                gst[j % 4][...], wd[cut, :],
                (((1,), (1,)), ((), ())), preferred_element_type=F32,
            )

    def dblock(q, j, half):
        return dpart[q % 4].at[pl.ds(pl.multiple_of(yat(j) * 64, 64), 64), pl.ds(half * 512, 512)]

    def dx_send(j):
        p = xat(j)
        send(f"da{j}", lambda: (dblock(j, 2, 0), dra[j % 4], dev(dy=1)))
        send(f"db{j}", lambda: (dblock(j, 2, 1), drb[j % 4], dev(dy=-1)))
        send(f"dc1{j}", lambda: (dblock(j, 1, 1), drc[j % 4][1], dev(dy=1)))
        send(f"dd0{j}", lambda: (dblock(j, -1, 0), drd[j % 4][0], dev(dy=-1)))

    def dx_middle(j):
        p = xat(j)
        recv(f"da{j}", dra[j % 4])
        dra[j % 4][...] += dblock(j, 1, 0)[...]
        send(f"dc0{j}", lambda: (dra[j % 4], drc[j % 4][0], dev(dy=1)))
        recv(f"db{j}", drb[j % 4])
        drb[j % 4][...] += dblock(j, -1, 1)[...]
        send(f"dd1{j}", lambda: (drb[j % 4], drd[j % 4][1], dev(dy=-1)))

    def dx_last(j):
        p = xat(j)
        for half in (1, 0):
            recv(f"dc{half}{j}", drc[j % 4][half])
            recv(f"dd{1 - half}{j}", drd[j % 4][1 - half])
        for half in range(2):
            dsum[j % 4][:, half * 512:half * 512 + 512] = (
                dblock(j, 0, half)[...] + drc[j % 4][half][...] + drd[j % 4][half][...]
            )

        @pl.when(p == zl)
        def _():
            dmine[...] = dsum[j % 4][...]

        @pl.when(p != zl)
        def _():
            slot = (zl - p + 4) % 4 - 1
            pltpu.make_async_remote_copy(
                dsum[j % 4], zrecv.at[slot], zss.at[slot], zrs.at[slot],
                device_id={"row": r, "col": p * 4 + y, "depth": d}, device_id_type=MESH,
            ).start()

    def x_stage(j):
        base = pl.multiple_of(d * 1024 + xat(j) * 256, 256)
        return pltpu.make_async_copy(xall.at[pl.ds(base, 256)], xst[j % 4], ls.at[4 + j % 4])

    def y_compute(j):
        x_stage(j).wait()

        @pl.loop(0, 7)
        def _(n):
            cut = pl.ds(pl.multiple_of(n * 256, 256), 256)
            ypart[j % 4][:, cut] = jnp.dot(
                xst[j % 4][...], wd[:, cut], preferred_element_type=F32
            )

        send(f"p{j}", lambda: (ypart[j % 4].at[pl.ds(pl.multiple_of((1 - k) * 128, 128), 128)], pair[j % 4], dev(dk=1)))

    def yblock(j, half):
        return pair[j % 4].at[:, pl.ds(half * 896, 896)]

    def y_pair(j):
        recv(f"p{j}", pair[j % 4])
        pair[j % 4][...] += ypart[j % 4][pl.ds(pl.multiple_of(k * 128, 128), 128), :]

    local[2].wait()
    tiles[56] = jnp.zeros((T, T), jnp.bfloat16)

    g_send("o", d, gout.at[0])
    z_send(0)
    y_send(0, act.at[0])

    def fill(i, at):
        for j in range(14):
            cell = i * 14 + j
            here = jnp.minimum(at, 55)
            hit = jnp.logical_and(at < 56, rows[0, 0, here] * 14 + cols[0, 0, here] == cell)
            wd[pl.ds(pl.multiple_of(i * T, T), T), j * T:j * T + T] = tiles[jnp.where(hit, at, 56)]
            at = at + hit.astype(jnp.int32)
        return at

    lax.fori_loop(0, 8, fill, jnp.int32(0))

    def dw_compute(dd, first):
        base = pl.multiple_of(dd * 1024, 1024)

        @pl.loop(0, 7)
        def _(n):
            cut = pl.ds(pl.multiple_of(n * 256, 256), 256)
            got = lax.dot_general(
                xall[pl.ds(base, 1024), :], gall[pl.ds(base, 1024), cut],
                (((0,), (0,)), ((), ())), preferred_element_type=F32,
            )
            for i in range(8):
                for j in range(2):
                    part = got[i * T:i * T + T, j * T:j * T + T]
                    at = i * 14 + n * 2 + j
                    dwd[at] = part if first else dwd[at] + part

    def out_send():
        send("oa", lambda: (yblock(2, 0), ya, dev(dx=1)))
        send("ob", lambda: (yblock(2, 1), yb, dev(dx=-1)))

    def out_middle():
        recv("oa", ya)
        ya[...] += yblock(1, 0)[...]
        send("oc0", lambda: (ya, yc[0], dev(dx=1)))
        recv("ob", yb)
        yb[...] += yblock(-1, 1)[...]
        send("od1", lambda: (yb, yd[1], dev(dx=-1)))

    z_recv(1)
    z_send(1)
    both(1, True, y_send)
    y_forward(0)
    local[1].wait()
    g_core("o", d, 0)
    dx_compute(0)
    z_recv(2)
    z_send(2)
    both(2, True, y_send)
    both(1, True, y_forward)
    z_recv(3)
    z_send(3)
    both(3, True, y_send)
    dx_send(0)
    send("gz0", lambda: (gout.at[0, pl.ds(0, 64)], gs(d, x, k, 0, 64), dev(dz=4)))
    send("gz1", lambda: (gout.at[0, pl.ds(64, 64)], gs(d, x, k, 64, 64), dev(dz=4)))
    both(2, True, y_forward)
    g_forward("o", d)
    g_core("o", d, 1)
    dx_compute(-1)
    g_core("o", d, 3)
    dx_compute(1)
    both(3, True, y_forward)
    dx_middle(0)
    dx_send(-1)
    dx_send(1)
    local[0].wait()
    y_last(0)
    for h in (1, 2, 3):
        both(h, True, y_last)
    for j in (2, 1, -1, 0):
        x_stage(j).start()
    y_compute(2)
    y_compute(1)
    y_pair(2)
    out_send()
    y_compute(-1)
    y_pair(1)
    send("oc1", lambda: (yblock(1, 1), yc[1], dev(dx=1)))
    y_pair(-1)
    send("od0", lambda: (yblock(-1, 0), yd[0], dev(dx=-1)))
    g_last("o", d)
    g_core("o", d, 2)
    dx_compute(2)
    dx_send(2)
    z_recv(4)
    for h in (1, 2, 3):
        both(h, False, y_send)
    y_send(4)
    y_compute(0)
    recv("gz0", gs(od, x, k, 0, 64))
    recv("gz1", gs(od, x, k, 64, 64))
    g_send("t", od, gs(od, x, k))
    dx_middle(-1)
    dx_middle(1)
    dw_compute(d, True)
    out_middle()
    for h in (1, 2, 3):
        both(h, False, y_forward)
    y_forward(4)
    dx_middle(2)
    g_forward("t", od)
    dx_last(0)
    dx_last(-1)
    dx_last(1)
    dx_last(2)
    for h in (1, 2, 3):
        both(h, False, y_last)
    y_last(4)
    y_pair(0)
    g_last("t", od)
    for j in range(4):
        g_core("t", od, j)
    dw_compute(od, False)

    scale = 1.0 / math.sqrt(2048.0)

    outs = []
    for part in range(4):
        for i in range(14):
            t = part * 14 + i
            dwt[part][i] = dwd[rows[0, 0, t] * 14 + cols[0, 0, t]] * scale
        out = pltpu.make_async_copy(dwt[part], dw_out.at[0, 0, pl.ds(part * 14, 14)], ls.at[12 + part])
        out.start()
        outs.append(out)
    for half in range(2):
        recv(f"oc{1 - half}", yc[1 - half])
        recv(f"od{half}", yd[half])
    for half in range(2):
        y_out[0, :, half * 896:half * 896 + 896] = (
            yblock(0, half)[...] + yc[half][...] + yd[half][...]
        ).astype(jnp.bfloat16)
    for slot in range(3):
        pltpu.make_async_remote_copy(
            zrecv.at[slot], zrecv.at[slot], zss.at[slot], zrs.at[slot],
            device_id=dev(dk=1), device_id_type=MESH,
        ).wait()
    dx_out[0] = (dmine[...] + zrecv[0] + zrecv[1] + zrecv[2]).astype(jnp.bfloat16)
    for out in outs:
        out.wait()
    for name, make in sent.items():
        desc(name, *make()).wait_send()


def hand_over(y_in, dx_in, dw_in, y_out, dx_out, dw_out, y_mid, dx_mid, dw_mid, sem):
    steps = [(y_in, y_mid, y_out), (dx_in, dx_mid, dx_out)]
    for i in range(4):
        cut = pl.ds(i * 14, 14)
        steps.append((dw_in.at[0, 0, cut], dw_mid.at[cut], dw_out.at[0, 0, cut]))
    into = [pltpu.make_async_copy(a, b, sem.at[0, i]) for i, (a, b, c) in enumerate(steps)]
    out = [pltpu.make_async_copy(b, c, sem.at[1, i]) for i, (a, b, c) in enumerate(steps)]
    for cp in into:
        cp.start()
    for first, second in zip(into, out):
        first.wait()
        second.start()
    for cp in out:
        cp.wait()


def shards(act, wt, rows, cols, gout):
    hbm = pl.BlockSpec(memory_space=pl.ANY)
    smem = pl.BlockSpec(memory_space=pltpu.SMEM)
    vmem = pl.BlockSpec(memory_space=pltpu.VMEM)
    bf16 = jnp.bfloat16
    dma = pltpu.SemaphoreType.DMA
    outs = [
        jax.ShapeDtypeStruct((1, 128, 1792), bf16),
        jax.ShapeDtypeStruct((1, 64, 1024), bf16),
        jax.ShapeDtypeStruct((1, 1, 56, T, T), F32),
    ]
    results = tuple(
        pl.pallas_call(
            kernel,
            out_shape=outs,
            in_specs=[hbm, hbm, smem, smem, hbm],
            out_specs=[vmem, vmem, hbm],
            scratch_shapes=[
                pltpu.VMEM((2048, 1024), bf16),
                pltpu.VMEM((2048, 1792), bf16),
                [pltpu.VMEM((256, 1024), bf16)] * 4,
                [pltpu.VMEM((256, 1792), bf16)] * 4,
                pltpu.VMEM((57, T, T), bf16),
                pltpu.VMEM((1024, 1792), bf16),
                pltpu.VMEM((112, T, T), F32),
                [pltpu.VMEM((14, T, T), F32)] * 4,
                [pltpu.VMEM((256, 1024), F32)] * 4,
                [pltpu.VMEM((64, 512), F32)] * 4,
                [pltpu.VMEM((64, 512), F32)] * 4,
                [[pltpu.VMEM((64, 512), F32)] * 2] * 4,
                [[pltpu.VMEM((64, 512), F32)] * 2] * 4,
                [pltpu.VMEM((64, 1024), F32)] * 4,
                pltpu.VMEM((64, 1024), F32),
                pltpu.VMEM((3, 64, 1024), F32),
                [pltpu.VMEM((256, 1792), F32)] * 4,
                [pltpu.VMEM((128, 1792), F32)] * 4,
                pltpu.VMEM((128, 896), F32),
                pltpu.VMEM((128, 896), F32),
                [pltpu.VMEM((128, 896), F32)] * 2,
                [pltpu.VMEM((128, 896), F32)] * 2,
                dma((NSEM,)), dma((NSEM,)), dma((16,)), dma((3,)), dma((3,)),
            ],
            compiler_params=pltpu.CompilerParams(
                collective_id=0, has_side_effects=True, vmem_limit_bytes=62 * 2**20
            ),
        )(act, wt, rows, cols, gout)
    )
    return tuple(
        pl.pallas_call(
            hand_over,
            out_shape=outs,
            in_specs=[hbm] * 3,
            out_specs=[hbm] * 3,
            scratch_shapes=[
                pltpu.VMEM((1, 128, 1792), bf16),
                pltpu.VMEM((1, 64, 1024), bf16),
                pltpu.VMEM((56, T, T), F32),
                dma((2, 6)),
            ],
            compiler_params=pltpu.CompilerParams(vmem_limit_bytes=60 * 2**20),
        )(*results)
    )


def solution(mesh):
    placed = (
        P("depth", "col", "row"),
        P("row", "col", None, None, None),
        P("row", "col", None),
        P("row", "col", None),
        P("depth", "row", "col"),
    )
    return jax.shard_map(
        shards,
        mesh=mesh,
        in_specs=placed,
        out_specs=(
            P("depth", "row", "col"),
            P("depth", "col", "row"),
            P("row", "col", None, None, None),
        ),
        check_vma=False,
    )
```
